32 devices in a mesh: groups: 1, ep: 32 (over z, y, x, core).
Axes of the slice: x: 2, y: 2, z: 4, core: 2. Of those that a mesh axis runs over, the one named last changes fastest.
Arguments:
- prefill_rows: bfloat16 [4096, 7168], P(('groups', 'ep')), may hold values from -6 to 6
- proj_weight: bfloat16 [7168, 576], P('ep'), may hold values from -0.0625 to 0.0625
- latent_gain: float32 [512], replicated, may hold values from 0.5 to 1.5
- prefill_position: int32 [4096], P(('groups', 'ep')), may hold values from 0 to 4095
- row_owner: int32 [4096, 1], P(('groups', 'ep')), may hold values from 0 to 31; in each aligned block of 128 rows (0 to 127, 128 to 255, ...) at most 8 rows name the same one
- row_request: int32 [4096], P(('groups', 'ep')), may hold values from 0 to 3
- latent_cache: bfloat16 [128, 256, 576], P(('groups', 'ep')), may hold values from -6 to 6
- cache_len: int32 [128], P(('groups', 'ep')), may hold values from 2 to 256, as said below
- queries: bfloat16 [4, 128, 64, 576], P(None, ('groups', 'ep')), may hold values from -60 to 60
- decode_rows: bfloat16 [4, 128, 7168], P(None, ('groups', 'ep')), may hold values from -6 to 6
- moe_gain: float32 [7168], replicated, may hold values from 0.5 to 1.5
- routes: int32 [4, 128, 2], P(None, ('groups', 'ep')), may hold values from 0 to 3, all different within a row; in each aligned block of 4 rows (0 to 3, 4 to 7, ..., all dimensions but the last counted through in order) at most 2 rows name the same one
- gate_scores: float32 [4, 128, 2], P(None, ('groups', 'ep')), may hold values from 0.1 to 1
- gate_weight: bfloat16 [7168, 4096], P(None, 'ep'), may hold values from -0.0625 to 0.0625
- up_weight: bfloat16 [7168, 4096], P(None, 'ep'), may hold values from -0.0625 to 0.0625
- down_weight: bfloat16 [4096, 7168], P('ep'), may hold values from -0.1875 to 0.1875
Outputs:
- attn_out: bfloat16 [4, 128, 64, 512], P(None, ('groups', 'ep'))
- moe_out: bfloat16 [4, 128, 7168], P(None, ('groups', 'ep'))
The draws below stay inside these ranges and needn't reach their ends.
Inputs may be any that keep to these rules, and one draw needn't show every extreme that they name: `row_owner`: among the 128 rows of one device, no owner is named more than 8 times, and one owner exactly that often. `routes`: among the 4 tokens of one device at one step, no expert is chosen more than 2 times, and one exactly that often. `cache_len`: some request has exactly 256 rows.
All inputs are finite; a program needn't handle non-finite values.
Results may differ from the reference program's by a relative error of at most 0.0071.
Values may be sent and summed in bfloat16 or wider, within the bound.
A program may use at most 128 MiB of HBM per device.

```python
import math
from functools import partial
import jax
import jax.numpy as jnp
import numpy as np
from jax import lax

D = 7168
KV_RANK = 512
ROPE = 64
HEADS = 64
MOE_FF = 1024
HID_DEV = 128
TOP = 2
STEPS = 4
PRE_DEV = 128
R_DEV = 4
CACHE = 256
EXPERTS = 4
CAP = 2
SEND_CAP = 8
TOKENS_PRE = 4096
REQUESTS = 128
N_EP = 32


def shared_rows(key):
    return jnp.clip(jax.random.normal(key, (REQUESTS, CACHE, KV_RANK + ROPE), jnp.float32), -6.0, 6.0)


def draw_latent_cache(key, part):
    base = shared_rows(key)
    return base.astype(jnp.bfloat16)


def draw_queries(key, part):
    key = jax.random.fold_in(key, 23)
    first = jax.random.fold_in(key, 0)
    noise = jax.random.normal(first, (STEPS, REQUESTS, HEADS, KV_RANK + ROPE), jnp.float32)
    return jnp.clip(noise, -6.0, 6.0).astype(jnp.bfloat16)


def draw_cache_len(key, part):
    key = jax.random.fold_in(key, 37)
    first, second = jax.random.split(key)
    lengths = jax.random.randint(first, (REQUESTS,), 2, CACHE + 1)
    peaked = jax.random.randint(second, (), 0, REQUESTS)
    return jnp.where(jnp.arange(REQUESTS) == peaked, CACHE, lengths).astype(jnp.int32)


def place_ends(array, rng, smallest, largest):
    extent = array.shape
    spot = [jax.random.randint(jax.random.fold_in(rng, axis), (), 0, extent[axis]) for axis in range(len(extent))]
    array = array.at[tuple(spot)].set(smallest)
    longest = extent.index(max(extent))
    spot[longest] = (spot[longest] + 1) % extent[longest]
    return array.at[tuple(spot)].set(largest)


def level_of(stream_key, dims, shards, low, top_value):
    def one(axis_at, shards_of):
        steps = jax.random.uniform(jax.random.fold_in(jax.random.fold_in(stream_key, 6), axis_at), (shards_of,), jnp.float32, low / len(shards), top_value / len(shards))
        return jnp.repeat(jnp.exp(steps), dims[axis_at] // shards_of).reshape((-1,) + (1,) * (len(dims) - axis_at - 1))

    factor_of = one(*shards[0])
    for cut in shards[1:]:
        factor_of = factor_of * one(*cut)
    return factor_of


def shared_out(own_key, own, number, rows, amount, top, reach, slope):
    ranking = jax.random.permutation(own_key, amount)
    crowded, ordinary = portions_of(amount, rows * top, reach, slope, True), portions_of(amount, rows * top, reach, slope, False)
    places = jnp.arange(amount)

    def named(sizes, turn):
        used = int((sizes > 0).sum())
        fixed = max(1, used // 4)
        moved = fixed + (places - fixed + turn * (used - fixed)) % max(1, amount - fixed)
        return jnp.zeros((amount,), jnp.int32).at[ranking[jnp.where(places < fixed, places, moved)]].set(jnp.asarray(sizes, jnp.int32))

    sizes = jnp.where(number % 4 == 0, named(crowded, number // 4), named(ordinary, number - number // 4 - 1))
    mixed = jax.random.permutation(jax.random.fold_in(own, 3), amount)
    source_of, taker = mixed[0:amount // 2 * 2:2], mixed[1:amount // 2 * 2:2]
    margin = jnp.minimum(sizes[source_of] - 1, reach - sizes[taker]) // 2
    margin = jnp.where((source_of == ranking[0]) | (taker == ranking[0]) | (sizes[taker] == 0), 0, jnp.maximum(margin, 0))
    moved = jax.random.randint(jax.random.fold_in(own, 4), (amount // 2,), 0, 1 << 20) % (margin + 1)
    sizes = sizes.at[source_of].add(-moved).at[taker].add(moved)
    members = jnp.searchsorted(jnp.cumsum(sizes), jnp.arange(rows * top), side="right").astype(jnp.int32)
    table = members.reshape(top, rows).T
    table = table[jax.random.permutation(jax.random.fold_in(own, 1), rows)]
    turn = jax.random.randint(jax.random.fold_in(own, 2), (rows, 1), 0, top)
    return jnp.take_along_axis(table, (jnp.arange(top)[None, :] + turn) % top, axis=1)


def portions_of(number_of, total, limit, lean, full):
    loads = [(1 << 20) // math.isqrt(rank ** lean) + 1 for rank in range(1, number_of + 1)]
    largest = limit if full else min(limit, max(-(-total // number_of), total * loads[0] // sum(loads)))
    least = 1 if total - largest >= number_of - 1 else 0
    holding, rest = [largest] + [least] * (number_of - 1), total - largest - least * (number_of - 1)
    while rest > 0:
        candidates = [i for i in range(1, number_of) if holding[i] < largest] or [i for i in range(1, number_of) if holding[i] < limit]
        pool, budget = sum([loads[i] for i in candidates]), rest
        for i in candidates:
            extra = min(limit - holding[i], max(1, budget * loads[i] // pool), rest)
            holding[i] = holding[i] + extra
            rest = rest - extra
    return np.array(holding)


def centred(stream_key, extent, deviation, most, shards=(), kind=jnp.bfloat16):
    values = deviation * jax.random.normal(stream_key, extent, jnp.float32)
    if shards:
        values = values * level_of(stream_key, extent, shards, -0.22, 0.18)
    return jnp.clip(values, -most, most).astype(kind)


def setup_inputs(seed: int = 0, part: int = 0) -> dict:
    seeds = jax.random.split(jax.random.key(seed), 17)
    part_splits = jax.random.split(jax.random.fold_in(seeds[16], part), 17)
    prefill_rows = centred(part_splits[0], (TOKENS_PRE, D), 1.0, 6.0, ((0, 32),))
    proj_weight = centred(seeds[1], (D, KV_RANK + ROPE), D ** -0.5, 0.0625, ((0, 32),))
    latent_gain = jnp.clip(1.0 + 0.1 * jax.random.normal(seeds[2], (KV_RANK,), jnp.float32), 0.5, 1.5)
    prefill_position = place_ends(jax.random.randint(part_splits[3], (TOKENS_PRE,), 0, 4096), jax.random.fold_in(part_splits[3], 1), 0, 4095).astype(jnp.int32)
    row_owner_keys = jax.random.split(jax.random.fold_in(part_splits[4], 1), TOKENS_PRE // PRE_DEV)
    row_owner_turns = jax.random.permutation(jax.random.fold_in(part_splits[4], 3), TOKENS_PRE // PRE_DEV)
    row_owner = jax.vmap(lambda own, number: shared_out(jax.random.fold_in(part_splits[4], 2), own, number, PRE_DEV, N_EP, 1, SEND_CAP, 2))(row_owner_keys, row_owner_turns).reshape((TOKENS_PRE, 1))
    row_request = place_ends(jax.random.randint(part_splits[5], (TOKENS_PRE,), 0, R_DEV), jax.random.fold_in(part_splits[5], 1), 0, R_DEV - 1).astype(jnp.int32)
    latent_cache = draw_latent_cache(jax.random.fold_in(jax.random.fold_in(seeds[16], part), 71), part)
    cache_len = draw_cache_len(jax.random.fold_in(jax.random.fold_in(seeds[16], part), 71), part)
    queries = draw_queries(jax.random.fold_in(jax.random.fold_in(seeds[16], part), 71), part)
    decode_rows = centred(part_splits[9], (STEPS, REQUESTS, D), 1.0, 6.0, ((1, 32),))
    moe_gain = jnp.clip(1.0 + 0.1 * jax.random.normal(seeds[10], (D,), jnp.float32), 0.5, 1.5)
    routes_keys = jax.random.split(jax.random.fold_in(part_splits[11], 1), STEPS * REQUESTS // R_DEV)
    routes_turns = jax.random.permutation(jax.random.fold_in(part_splits[11], 3), STEPS * REQUESTS // R_DEV)
    routes = jax.vmap(lambda own, number: shared_out(jax.random.fold_in(part_splits[11], 2), own, number, R_DEV, EXPERTS, TOP, CAP, 2))(routes_keys, routes_turns).reshape((STEPS, REQUESTS, TOP))
    gate_scores = jnp.clip(0.1 + 0.9 * jax.random.uniform(part_splits[12], (STEPS, REQUESTS, TOP), jnp.float32) ** level_of(part_splits[12], (STEPS, REQUESTS, TOP), ((1, 32),), -0.2, 0.2), 0.1, 1.0)
    gate_weight = centred(seeds[13], (D, EXPERTS * MOE_FF), D ** -0.5, 0.0625, ((1, 32),))
    up_weight = centred(seeds[14], (D, EXPERTS * MOE_FF), D ** -0.5, 0.0625, ((1, 32),))
    down_weight = centred(seeds[15], (EXPERTS * MOE_FF, D), MOE_FF ** -0.5, 0.1875, ((0, 32),))
    return {"prefill_rows": prefill_rows, "proj_weight": proj_weight, "latent_gain": latent_gain, "prefill_position": prefill_position, "row_owner": row_owner, "row_request": row_request, "latent_cache": latent_cache, "cache_len": cache_len, "queries": queries, "decode_rows": decode_rows, "moe_gain": moe_gain, "routes": routes, "gate_scores": gate_scores, "gate_weight": gate_weight, "up_weight": up_weight, "down_weight": down_weight}


NORM_EPS = 1e-06
SOFT_SCALE = 192.0 ** (-0.5)
NEG_FILL = -1e+30

def latent_rows(projected, positions, latent_gain):
    compressed = projected[:, :KV_RANK]
    rotary = projected[:, KV_RANK:]
    factor = lax.rsqrt(lax.optimization_barrier(jnp.mean(compressed * compressed, axis=1, keepdims=True)) + NORM_EPS)
    compressed = compressed * factor * latent_gain.astype(jnp.float32)[None, :]
    half_width = rotary.shape[1] // 2
    frequency = 10000.0 ** (-jnp.arange(half_width, dtype=jnp.float32) / half_width)
    angles = positions.astype(jnp.float32)[:, None] * frequency[None, :]
    cosine = jnp.cos(angles)
    sine_part = jnp.sin(angles)
    first_half = rotary[:, :half_width]
    second_half = rotary[:, half_width:]
    rotated = jnp.concatenate([first_half * cosine - second_half * sine_part, second_half * cosine + first_half * sine_part], axis=1)
    return jnp.concatenate([compressed, rotated], axis=1).astype(jnp.bfloat16)

def place_rows(destination, local_request, payload, dest_count, capacity):
    dest_ids = jnp.arange(dest_count, dtype=jnp.int32)
    onehot = (destination[:, None] == dest_ids[None, :]).astype(jnp.int32)
    earlier = jnp.cumsum(onehot, axis=0) - onehot
    target = destination * capacity + lax.optimization_barrier(jnp.sum(earlier * onehot, axis=1))
    select = jnp.arange(dest_count * capacity, dtype=jnp.int32)[:, None] == target[None, :]
    placed = jnp.dot(select.astype(jnp.bfloat16), payload, preferred_element_type=jnp.float32).astype(jnp.bfloat16)
    labels = lax.optimization_barrier(jnp.sum(select.astype(jnp.int32) * (local_request[None, :] + 1), axis=1)) - 1
    return (placed.reshape(dest_count, capacity, payload.shape[1]), labels.reshape(dest_count, capacity))

def attend(queries, cache_rows, lengths, received, labels, own_rows):
    step_count, req_count = (queries.shape[0], queries.shape[1])
    query_wide = queries.astype(jnp.float32)
    cache_wide = cache_rows.astype(jnp.float32)
    recv_wide = received.astype(jnp.float32)
    own_wide = own_rows.astype(jnp.float32)
    score_cache = jnp.einsum('trhc,rkc->trhk', query_wide, cache_wide) * SOFT_SCALE
    score_recv = jnp.einsum('trhc,mc->trhm', query_wide, recv_wide) * SOFT_SCALE
    score_own = jnp.einsum('trhc,src->trhs', query_wide, own_wide) * SOFT_SCALE
    mask_cache = (jnp.arange(cache_rows.shape[1], dtype=jnp.int32)[None, :] < lengths[:, None])[None, :, None, :]
    mask_recv = (labels[None, :] == jnp.arange(req_count, dtype=jnp.int32)[:, None])[None, :, None, :]
    step_ids = jnp.arange(step_count, dtype=jnp.int32)
    mask_own = (step_ids[None, :] <= step_ids[:, None])[:, None, None, :]
    score_cache = jnp.where(mask_cache, score_cache, NEG_FILL)
    score_recv = jnp.where(mask_recv, score_recv, NEG_FILL)
    score_own = jnp.where(mask_own, score_own, NEG_FILL)
    highest = jnp.maximum(jnp.maximum(score_cache.max(axis=-1), score_recv.max(axis=-1)), score_own.max(axis=-1))[..., None]
    exp_cache = jnp.where(mask_cache, jnp.exp(score_cache - highest), 0.0)
    exp_recv = jnp.where(mask_recv, jnp.exp(score_recv - highest), 0.0)
    exp_own = jnp.where(mask_own, jnp.exp(score_own - highest), 0.0)
    denominator = exp_cache.sum(axis=-1, keepdims=True) + exp_recv.sum(axis=-1, keepdims=True) + exp_own.sum(axis=-1, keepdims=True)
    prob_cache = (exp_cache / denominator).astype(jnp.bfloat16).astype(jnp.float32)
    prob_recv = (exp_recv / denominator).astype(jnp.bfloat16).astype(jnp.float32)
    prob_own = (exp_own / denominator).astype(jnp.bfloat16).astype(jnp.float32)
    result = jnp.einsum('trhk,rkc->trhc', prob_cache, cache_wide[:, :, :KV_RANK])
    result = result + jnp.einsum('trhm,mc->trhc', prob_recv, recv_wide[:, :KV_RANK])
    result = result + jnp.einsum('trhs,src->trhc', prob_own, own_wide[:, :, :KV_RANK])
    return result.astype(jnp.bfloat16)

def attend_packed(packed):
    return attend(packed[0], packed[1], packed[2], packed[3], packed[4], packed[5])

def reference(prefill_rows, proj_weight, latent_gain, prefill_position, row_owner, row_request, latent_cache, cache_len, queries, decode_rows, moe_gain, routes, gate_scores, gate_weight, up_weight, down_weight):
    latent_width = KV_RANK + ROPE
    model_width = prefill_rows.shape[1]
    prefill_latent = latent_rows(jnp.dot(prefill_rows, proj_weight, preferred_element_type=jnp.float32), prefill_position, latent_gain)
    step_ids = jnp.arange(STEPS, dtype=jnp.int32)
    decode_position = (cache_len[None, :] + step_ids[:, None]).reshape(-1)
    flat_decode = decode_rows.reshape(STEPS * REQUESTS, model_width)
    decode_latent = latent_rows(jnp.dot(flat_decode, proj_weight, preferred_element_type=jnp.float32), decode_position, latent_gain)
    decode_latent = decode_latent.reshape(STEPS, REQUESTS, latent_width)
    placer = jax.vmap(partial(place_rows, dest_count=N_EP, capacity=SEND_CAP))
    placed, labels = placer(row_owner[:, 0].reshape(N_EP, PRE_DEV), row_request.reshape(N_EP, PRE_DEV), prefill_latent.reshape(N_EP, PRE_DEV, latent_width))
    received = jnp.swapaxes(placed, 0, 1).reshape(N_EP, N_EP * SEND_CAP, latent_width)
    received_labels = jnp.swapaxes(labels, 0, 1).reshape(N_EP, N_EP * SEND_CAP)
    owner_queries = jnp.moveaxis(queries.reshape(STEPS, N_EP, R_DEV, HEADS, latent_width), 1, 0)
    owner_rows = jnp.moveaxis(decode_latent.reshape(STEPS, N_EP, R_DEV, latent_width), 1, 0)
    attended = lax.map(attend_packed, (owner_queries, latent_cache.reshape(N_EP, R_DEV, CACHE, latent_width), cache_len.reshape(N_EP, R_DEV), received, received_labels, owner_rows))
    attn_out = jnp.moveaxis(attended, 0, 1).reshape(STEPS, REQUESTS, HEADS, KV_RANK)
    token_rows = flat_decode.astype(jnp.float32)
    factor = lax.rsqrt(lax.optimization_barrier(jnp.mean(token_rows * token_rows, axis=1, keepdims=True)) + NORM_EPS)
    normed = (token_rows * factor * moe_gain.astype(jnp.float32)[None, :]).astype(jnp.bfloat16)
    split_count = MOE_FF // HID_DEV
    flat_routes = routes.reshape(-1, TOP)
    flat_gates = gate_scores.reshape(-1, TOP).astype(jnp.float32)
    token_count = normed.shape[0]

    def expert_output(expert):

        def add_slice(total, slice_at):
            column = (expert * split_count + slice_at) * HID_DEV
            gate_part = lax.dynamic_slice_in_dim(gate_weight, column, HID_DEV, 1)
            up_part = lax.dynamic_slice_in_dim(up_weight, column, HID_DEV, 1)
            down_part = lax.dynamic_slice_in_dim(down_weight, column, HID_DEV, 0)
            hidden = (jax.nn.silu(jnp.dot(normed, gate_part, preferred_element_type=jnp.float32)) * jnp.dot(normed, up_part, preferred_element_type=jnp.float32)).astype(jnp.bfloat16)
            partial_out = jnp.dot(hidden, down_part, preferred_element_type=jnp.float32).astype(jnp.bfloat16)
            return (total + partial_out.astype(jnp.float32), None)
        total, _ = lax.scan(add_slice, jnp.zeros((token_count, model_width), jnp.float32), jnp.arange(split_count, dtype=jnp.int32))
        return total

    def add_expert(accum, expert):
        weight = lax.optimization_barrier(jnp.sum(jnp.where(flat_routes == expert, flat_gates, 0.0), axis=1))
        return (accum + weight[:, None] * expert_output(expert), None)
    accum, _ = lax.scan(add_expert, jnp.zeros((token_count, model_width), jnp.float32), jnp.arange(EXPERTS, dtype=jnp.int32))
    moe_out = accum.astype(jnp.bfloat16).reshape(STEPS, REQUESTS, model_width)
    return (attn_out, moe_out)
```

```python
import functools

import jax
import jax.numpy as jnp
from jax import lax
from jax.experimental import pallas as pl
from jax.experimental.pallas import tpu as pltpu
from jax.sharding import PartitionSpec as P

KV_RANK = 512
MOE_FF = 1024
TOP = 2


NORM_EPS = 1e-06
SOFT_SCALE = 192.0 ** (-0.5)
NEG_FILL = -1e30


def latent_rows(projected, positions, latent_gain):
    compressed = projected[:, :KV_RANK]
    rotary = projected[:, KV_RANK:]
    factor = lax.rsqrt(jnp.mean(compressed * compressed, axis=1, keepdims=True) + NORM_EPS)
    compressed = compressed * factor * latent_gain[None, :]
    half_width = rotary.shape[1] // 2
    frequency = 10000.0 ** (-jnp.arange(half_width, dtype=jnp.float32) / half_width)
    angles = positions.astype(jnp.float32)[:, None] * frequency[None, :]
    cosine = jnp.cos(angles)
    sine_part = jnp.sin(angles)
    first_half = rotary[:, :half_width]
    second_half = rotary[:, half_width:]
    rotated = jnp.concatenate(
        [
            first_half * cosine - second_half * sine_part,
            second_half * cosine + first_half * sine_part,
        ],
        axis=1,
    )
    return jnp.concatenate([compressed, rotated], axis=1).astype(jnp.bfloat16)


def attend(queries, cache_rows, lengths, received, labels, own_rows):
    step_count, req_count = (queries.shape[0], queries.shape[1])
    score_cache = (
        jnp.einsum("trhc,rkc->trhk", queries, cache_rows, preferred_element_type=jnp.float32)
        * SOFT_SCALE
    )
    score_recv = (
        jnp.einsum("trhc,mc->trhm", queries, received, preferred_element_type=jnp.float32)
        * SOFT_SCALE
    )
    score_own = (
        jnp.einsum("trhc,src->trhs", queries, own_rows, preferred_element_type=jnp.float32)
        * SOFT_SCALE
    )
    mask_cache = (jnp.arange(cache_rows.shape[1], dtype=jnp.int32)[None, :] < lengths[:, None])[
        None, :, None, :
    ]
    mask_recv = (labels[None, :] == jnp.arange(req_count, dtype=jnp.int32)[:, None])[
        None, :, None, :
    ]
    step_ids = jnp.arange(step_count, dtype=jnp.int32)
    mask_own = (step_ids[None, :] <= step_ids[:, None])[:, None, None, :]
    score_cache = jnp.where(mask_cache, score_cache, NEG_FILL)
    score_recv = jnp.where(mask_recv, score_recv, NEG_FILL)
    score_own = jnp.where(mask_own, score_own, NEG_FILL)
    highest = jnp.maximum(
        jnp.maximum(score_cache.max(axis=-1), score_recv.max(axis=-1)), score_own.max(axis=-1)
    )[..., None]
    exp_cache = jnp.where(mask_cache, jnp.exp(score_cache - highest), 0.0)
    exp_recv = jnp.where(mask_recv, jnp.exp(score_recv - highest), 0.0)
    exp_own = jnp.where(mask_own, jnp.exp(score_own - highest), 0.0)
    denominator = (
        exp_cache.sum(axis=-1, keepdims=True)
        + exp_recv.sum(axis=-1, keepdims=True)
        + exp_own.sum(axis=-1, keepdims=True)
    )
    prob_cache = (exp_cache / denominator).astype(jnp.bfloat16)
    prob_recv = (exp_recv / denominator).astype(jnp.bfloat16)
    prob_own = (exp_own / denominator).astype(jnp.bfloat16)
    result = jnp.einsum(
        "trhk,rkc->trhc", prob_cache, cache_rows[:, :, :KV_RANK], preferred_element_type=jnp.float32
    )
    result = result + jnp.einsum(
        "trhm,mc->trhc", prob_recv, received[:, :KV_RANK], preferred_element_type=jnp.float32
    )
    result = result + jnp.einsum(
        "trhs,src->trhc", prob_own, own_rows[:, :, :KV_RANK], preferred_element_type=jnp.float32
    )
    return result.astype(jnp.bfloat16)


PLANE = 8
SLAB = 16
TILE = 512


def place_rows(destination, payload, dest_count, capacity):
    dest_ids = jnp.arange(dest_count, dtype=jnp.int32)
    onehot = (destination[:, None] == dest_ids[None, :]).astype(jnp.int32)
    earlier = jnp.cumsum(onehot, axis=0) - onehot
    target = destination * capacity + jnp.sum(earlier * onehot, axis=1)
    select = jnp.arange(dest_count * capacity, dtype=jnp.int32)[:, None] == target[None, :]
    placed = jnp.dot(
        select.astype(jnp.bfloat16), payload, preferred_element_type=jnp.float32
    ).astype(jnp.bfloat16)
    return placed.reshape(dest_count, capacity, payload.shape[1])


def exchange_kernel(
    expert_count,
    w_ref, tok_ref, pre_hbm, dec_ref, gate_hbm, up_hbm, down_hbm,
    proj_ref, back_ref,
    weight, tokens, pre, gate, up, down, accum, hidden, part,
    from_sib, from_a, from_b, sum_a, sum_d, own_sum, sum_b, total, back,
    zs, zr, ps, pr, local, ss, sr, as_, ar, bs, br, fs, fr,
):
    E = expert_count
    me = lax.axis_index("ep")
    e0 = me // PLANE
    j = me % PLANE
    b0, b1, b2 = j % 2, (j // 2) % 2, j // 4
    dx = 2 - 4 * b1
    dy = 4 - 8 * b2
    ds = 1 - 2 * b0
    da = dx * (1 - b0) + dy * b0
    db = dx * b0 + dy * (1 - b0)
    jS, jA, jB, jD = j + ds, j + da, j + db, j + dx + dy
    sA, sB, sD = jS + db, jS + da, jS + dx + dy
    base = e0 * PLANE
    half = tok_ref.shape[2]

    def remote(src, dst, send, recv, device):
        return pltpu.make_async_remote_copy(
            src_ref=src, dst_ref=dst, send_sem=send, recv_sem=recv,
            device_id={"ep": device}, device_id_type=pl.DeviceIdType.MESH,
        )

    loads = [
        pltpu.make_async_copy(w_ref, weight.at[e0, j], local.at[0]),
        pltpu.make_async_copy(tok_ref.at[e0], tokens.at[e0, j], local.at[1]),
        pltpu.make_async_copy(gate_hbm, gate, local.at[2]),
        pltpu.make_async_copy(up_hbm, up, local.at[3]),
        pltpu.make_async_copy(pre_hbm, pre, local.at[4]),
        pltpu.make_async_copy(down_hbm, down, local.at[5]),
    ]
    for load in loads:
        load.start()

    barrier = pltpu.get_barrier_semaphore()
    for k in range(1, E):
        pl.semaphore_signal(
            barrier, inc=1, device_id={"ep": ((e0 + k) % E) * PLANE + j},
            device_id_type=pl.DeviceIdType.MESH,
        )
    for peer in (jS, jA, jB):
        pl.semaphore_signal(
            barrier, inc=1, device_id={"ep": base + peer},
            device_id_type=pl.DeviceIdType.MESH,
        )
    pl.semaphore_wait(barrier, E - 1 + 3)

    def column_send(kind, e):
        source = tok_ref.at[e] if kind == 0 else w_ref
        buffer = tokens if kind == 0 else weight
        return remote(
            source, buffer.at[e0, j], zs.at[kind, e], zr.at[kind, e0], e * PLANE + j
        )

    def column_recv(kind, e):
        source = tok_ref.at[e] if kind == 0 else w_ref
        buffer = tokens if kind == 0 else weight
        return remote(
            source, buffer.at[e, j], zs.at[kind, e], zr.at[kind, e], e * PLANE + j
        )

    for k in range(1, E):
        e = (e0 + k) % E
        column_send(0, e).start()
        column_send(1, e).start()
    loads[0].wait()
    loads[1].wait()

    def plane_send(kind, e, which):
        buffer = tokens if kind == 0 else weight
        block = (j, j, j, jA, jA, jB, jD)[which]
        peer = (jA, jB, jS, jB, jS, jS, jS)[which]
        ref = buffer.at[e, block]
        return remote(ref, ref, ps.at[kind, e, which], pr.at[kind, e, which], base + peer)

    def plane_recv(kind, e, which):
        buffer = tokens if kind == 0 else weight
        block = (jA, jB, jS, jD, sA, sB, sD)[which]
        peer = (jA, jB, jS, jB, jS, jS, jS)[which]
        ref = buffer.at[e, block]
        return remote(ref, ref, ps.at[kind, e, which], pr.at[kind, e, which], base + peer)

    def expert_in(e):
        @pl.loop(0, half // TILE)
        def _(t):
            first = pl.multiple_of(t * TILE, TILE)
            second = pl.multiple_of(half + t * TILE, TILE)
            x = tokens[e, :, :, pl.ds(first, TILE)].reshape(PLANE * SLAB, TILE)
            for at, (matrix, start) in enumerate(
                ((gate, first), (gate, second), (up, first), (up, second))
            ):
                product = jnp.dot(
                    x, matrix[pl.ds(start, TILE), :], preferred_element_type=jnp.float32
                )
                accum[at] = jnp.where(t == 0, 0.0, accum[at]) + product

        def joined(at):
            low = accum[at].reshape(PLANE, SLAB, -1)[:, : SLAB // 2]
            high = accum[at + 1].reshape(PLANE, SLAB, -1)[:, SLAB // 2 :]
            return (low + high).reshape(PLANE * SLAB // 2, -1)

        hidden[e] = (jax.nn.silu(joined(0)) * joined(2)).astype(jnp.bfloat16)

    loads[2].wait()
    loads[3].wait()

    @pl.loop(0, E + 3)
    def _(t):
        @pl.when(t < E)
        def _():
            e = (e0 + t) % E
            for kind in (0, 1):
                @pl.when(t > 0)
                def _():
                    column_recv(kind, e).wait_recv()
                for which in (0, 1, 2):
                    plane_send(kind, e, which).start()

        @pl.when((t >= 1) & (t < E + 1))
        def _():
            e = (e0 + t - 1) % E
            for kind in (0, 1):
                plane_recv(kind, e, 0).wait_recv()
                plane_send(kind, e, 3).start()
                plane_send(kind, e, 4).start()
                plane_recv(kind, e, 1).wait_recv()
                plane_send(kind, e, 5).start()

        @pl.when((t >= 2) & (t < E + 2))
        def _():
            e = (e0 + t - 2) % E
            for kind in (0, 1):
                plane_recv(kind, e, 3).wait_recv()
                plane_send(kind, e, 6).start()

        @pl.when(t >= 3)
        def _():
            e = (e0 + t - 3) % E
            for which in (2, 4, 5, 6):
                plane_recv(0, e, which).wait_recv()
            expert_in(e)

    loads[4].wait()
    loads[5].wait()

    def project():
        pre_count = pre.shape[0]
        depth = pre.shape[1] // E

        @pl.loop(0, E)
        def _(e):
            for which in (2, 4, 5, 6):
                plane_recv(1, e, which).wait_recv()

        @pl.loop(0, E)
        def _(e):
            block = weight[e].reshape(depth, -1)
            columns = pl.ds(pl.multiple_of(e * depth, 128), depth)
            for rows, offset in ((pre, 0), (dec_ref, pre_count)):
                place = pl.ds(offset, rows.shape[0])
                product = jnp.dot(
                    rows[:, columns], block, preferred_element_type=jnp.float32
                )
                proj_ref[place, :] = jnp.where(e == 0, 0.0, proj_ref[place, :]) + product

    def sib_send(e, which):
        block = (jS, sA, sB, sD)[which]
        return remote(
            part.at[e, block], from_sib.at[e, which], ss.at[e, which], sr.at[e, which], base + jS
        )

    def a_send(e, which):
        source = (sum_a, sum_d)[which]
        return remote(
            source.at[e], from_a.at[e, which], as_.at[e, which], ar.at[e, which], base + jA
        )

    def b_send(e):
        return remote(sum_b.at[e], from_b.at[e], bs.at[e], br.at[e], base + jB)

    def back_send(e):
        return remote(total.at[e], back.at[e0], fs.at[e], fr.at[e0], e * PLANE + j)

    def back_recv(e):
        return remote(total.at[e], back.at[e], fs.at[e], fr.at[e], e * PLANE + j)

    def wide(ref):
        return ref.astype(jnp.float32)

    @pl.loop(0, E + 3)
    def _(t):
        @pl.when(t < E)
        def _():
            e = (e0 + 1 + t) % E

            @pl.loop(0, half // TILE)
            def _(c):
                first = pl.multiple_of(c * TILE, TILE)
                second = pl.multiple_of(half + c * TILE, TILE)
                low, high = (
                    jnp.dot(
                        hidden[e], down[:, pl.ds(start, TILE)],
                        preferred_element_type=jnp.float32,
                    ).reshape(PLANE, SLAB // 2, TILE)
                    for start in (first, second)
                )
                part[e, :, :, pl.ds(first, TILE)] = jnp.concatenate([low, high], axis=1).astype(
                    jnp.bfloat16
                )

            for which in range(4):
                sib_send(e, which).start()

        @pl.when((t >= 1) & (t < E + 1))
        def _():
            e = (e0 + t) % E
            sib_send(e, 1).wait_recv()
            sum_a[e] = (wide(part[e, jA]) + wide(from_sib[e, 1])).astype(jnp.bfloat16)
            a_send(e, 0).start()
            sib_send(e, 3).wait_recv()
            sum_d[e] = (wide(part[e, jD]) + wide(from_sib[e, 3])).astype(jnp.bfloat16)
            a_send(e, 1).start()

        @pl.when((t >= 2) & (t < E + 2))
        def _():
            e = (e0 + t - 1) % E
            sib_send(e, 0).wait_recv()
            sib_send(e, 2).wait_recv()
            a_send(e, 1).wait_recv()
            sum_b[e] = (
                wide(part[e, jB]) + wide(from_sib[e, 2]) + wide(from_a[e, 1])
            ).astype(jnp.bfloat16)
            b_send(e).start()
            a_send(e, 0).wait_recv()
            own_sum[e] = wide(part[e, j]) + wide(from_sib[e, 0]) + wide(from_a[e, 0])

        @pl.when(t >= 3)
        def _():
            e = (e0 + t - 2) % E
            b_send(e).wait_recv()
            total[e] = (own_sum[e] + wide(from_b[e])).astype(jnp.bfloat16)

            @pl.when(t < E + 2)
            def _():
                back_send(e).start()

        @pl.when(t == 1)
        def _():
            project()

    back_ref[e0] = wide(total[e0])

    @pl.loop(1, E)
    def _(k):
        e = (e0 + k) % E
        back_recv(e).wait_recv()
        back_ref[e] = wide(back[e])

    @pl.loop(0, E)
    def _(e):
        for kind in (0, 1):
            for which in range(7):
                plane_send(kind, e, which).wait_send()
        for which in range(4):
            sib_send(e, which).wait_send()
        a_send(e, 0).wait_send()
        a_send(e, 1).wait_send()
        b_send(e).wait_send()

    @pl.loop(1, E)
    def _(k):
        e = (e0 + k) % E
        column_send(0, e).wait_send()
        column_send(1, e).wait_send()
        back_send(e).wait_send()


def exchange(proj_weight, packed, prefill_rows, decode_flat, gate_weight, up_weight, down_weight):
    E, _, half = packed.shape
    width = 2 * half
    shard, latent_width = proj_weight.shape
    hidden_dev = gate_weight.shape[1]
    rows = prefill_rows.shape[0] + decode_flat.shape[0]
    bf16 = jnp.bfloat16
    block = (E, SLAB, half)
    dma = pltpu.SemaphoreType.DMA
    vmem = pl.BlockSpec(memory_space=pltpu.VMEM)
    hbm = pl.BlockSpec(memory_space=pl.ANY)
    return pl.pallas_call(
        functools.partial(exchange_kernel, E),
        out_shape=(
            jax.ShapeDtypeStruct((rows, latent_width), jnp.float32),
            jax.ShapeDtypeStruct(block, jnp.float32),
        ),
        in_specs=[vmem, vmem, hbm, vmem, hbm, hbm, hbm],
        out_specs=(vmem, vmem),
        scratch_shapes=[
            pltpu.VMEM((E, PLANE, shard, latent_width), bf16),
            pltpu.VMEM((E, PLANE, SLAB, half), bf16),
            pltpu.VMEM(prefill_rows.shape, bf16),
            pltpu.VMEM(gate_weight.shape, bf16),
            pltpu.VMEM(up_weight.shape, bf16),
            pltpu.VMEM(down_weight.shape, bf16),
            pltpu.VMEM((4, PLANE * SLAB, hidden_dev), jnp.float32),
            pltpu.VMEM((E, PLANE * SLAB // 2, hidden_dev), bf16),
            pltpu.VMEM((E, PLANE, SLAB, half), bf16),
            pltpu.VMEM((E, 4, SLAB, half), bf16),
            pltpu.VMEM((E, 2, SLAB, half), bf16),
            pltpu.VMEM(block, bf16),
            pltpu.VMEM(block, bf16),
            pltpu.VMEM(block, bf16),
            pltpu.VMEM(block, jnp.float32),
            pltpu.VMEM(block, bf16),
            pltpu.VMEM(block, bf16),
            pltpu.VMEM(block, bf16),
            dma((2, E)), dma((2, E)), dma((2, E, 7)), dma((2, E, 7)), dma((6,)),
            dma((E, 4)), dma((E, 4)), dma((E, 2)), dma((E, 2)), dma((E,)), dma((E,)),
            dma((E,)), dma((E,)),
        ],
        compiler_params=pltpu.CompilerParams(
            collective_id=0, has_side_effects=True, vmem_limit_bytes=56 * 1024 * 1024
        ),
    )(proj_weight, packed, prefill_rows, decode_flat, gate_weight, up_weight, down_weight)


def pack(normed, routes, gate_scores, expert_count, capacity):
    step_count, req_count, width = normed.shape
    chosen = routes.reshape(step_count, req_count * TOP)
    onehot = (chosen[:, :, None] == jnp.arange(expert_count, dtype=jnp.int32)).astype(jnp.int32)
    earlier = jnp.cumsum(onehot, axis=1) - onehot
    slots = step_count * capacity
    step_ids = jnp.arange(step_count, dtype=jnp.int32)[:, None]
    row = chosen * slots + step_ids * capacity + jnp.sum(earlier * onehot, axis=2)
    row = row.reshape(step_count * req_count, TOP)
    match = row[:, :, None] == jnp.arange(expert_count * slots, dtype=jnp.int32)
    mixing = jnp.sum(jnp.where(match, gate_scores.reshape(-1, TOP)[:, :, None], 0.0), axis=1)
    select = jnp.any(match, axis=1).astype(jnp.bfloat16)
    packed = jnp.einsum(
        "tr,td->rd", select, normed.reshape(-1, width), preferred_element_type=jnp.float32
    ).astype(jnp.bfloat16)
    packed = packed.reshape(expert_count, slots, 2, width // 2).transpose(0, 2, 1, 3)
    return packed.reshape(expert_count, 2 * slots, width // 2), mixing


def shards(
    prefill_rows,
    proj_weight,
    latent_gain,
    prefill_position,
    row_owner,
    row_request,
    latent_cache,
    cache_len,
    queries,
    decode_rows,
    moe_gain,
    routes,
    gate_scores,
    gate_weight,
    up_weight,
    down_weight,
):
    ep_count = lax.axis_size("ep")
    pre_count = prefill_rows.shape[0]
    step_count, req_count, width = decode_rows.shape
    latent_width = proj_weight.shape[1]
    expert_count = ep_count // PLANE
    assert MOE_FF == PLANE * gate_weight.shape[1]
    capacity = max(2, req_count * TOP // expert_count)
    assert step_count * capacity * 2 == SLAB

    token_rows = decode_rows.astype(jnp.float32)
    factor = lax.rsqrt(jnp.mean(token_rows * token_rows, axis=2, keepdims=True) + NORM_EPS)
    normed = (token_rows * factor * moe_gain[None, None, :]).astype(jnp.bfloat16)
    packed, mixing = pack(normed, routes, gate_scores, expert_count, capacity)

    projected, back = exchange(
        proj_weight,
        packed,
        prefill_rows,
        decode_rows.reshape(step_count * req_count, width),
        gate_weight,
        up_weight,
        down_weight,
    )

    decode_position = (
        cache_len[None, :] + jnp.arange(step_count, dtype=jnp.int32)[:, None]
    ).reshape(-1)
    positions = jnp.concatenate([prefill_position, decode_position], axis=0)
    latent = latent_rows(projected, positions, latent_gain)
    own_rows = latent[pre_count:].reshape(step_count, req_count, latent_width)
    send_cap = max(2, 2 * pre_count // ep_count)
    payload = jnp.concatenate(
        [latent[:pre_count], (row_request + 1).astype(jnp.bfloat16)[:, None]], axis=1
    )
    placed = place_rows(row_owner[:, 0], payload, ep_count, send_cap)
    received = lax.all_to_all(placed, "ep", split_axis=0, concat_axis=0, tiled=True)
    received = received.reshape(-1, latent_width + 1)
    attn_out = attend(
        queries,
        latent_cache,
        cache_len,
        received[:, :latent_width],
        received[:, latent_width].astype(jnp.int32) - 1,
        own_rows,
    )
    slots = step_count * capacity
    expert_rows = back.reshape(expert_count, 2, slots, width // 2).transpose(0, 2, 1, 3)
    moe_out = jnp.dot(
        mixing,
        expert_rows.reshape(expert_count * slots, width),
        precision=lax.Precision.HIGHEST,
        preferred_element_type=jnp.float32,
    )
    moe_out = moe_out.reshape(step_count, req_count, width).astype(jnp.bfloat16)
    return (attn_out, moe_out)


def solution(mesh):
    in_specs = (
        P(("groups", "ep"), None),
        P("ep", None),
        P(),
        P(("groups", "ep")),
        P(("groups", "ep"), None),
        P(("groups", "ep")),
        P(("groups", "ep"), None, None),
        P(("groups", "ep")),
        P(None, ("groups", "ep"), None, None),
        P(None, ("groups", "ep"), None),
        P(),
        P(None, ("groups", "ep"), None),
        P(None, ("groups", "ep"), None),
        P(None, "ep"),
        P(None, "ep"),
        P("ep", None),
    )
    out_specs = (P(None, ("groups", "ep"), None, None), P(None, ("groups", "ep"), None))
    return jax.shard_map(shards, mesh=mesh, in_specs=in_specs, out_specs=out_specs, check_vma=False)
```

```python
import functools

import jax
import jax.numpy as jnp
from jax import lax
from jax.experimental import pallas as pl
from jax.experimental.pallas import tpu as pltpu
from jax.sharding import PartitionSpec as P

KV_RANK = 512
MOE_FF = 1024
TOP = 2


NORM_EPS = 1e-06
SOFT_SCALE = 192.0 ** (-0.5)
NEG_FILL = -1e30


def latent_rows(projected, positions, latent_gain):
    compressed = projected[:, :KV_RANK]
    rotary = projected[:, KV_RANK:]
    factor = lax.rsqrt(jnp.mean(compressed * compressed, axis=1, keepdims=True) + NORM_EPS)
    compressed = compressed * factor * latent_gain[None, :]
    half_width = rotary.shape[1] // 2
    frequency = 10000.0 ** (-jnp.arange(half_width, dtype=jnp.float32) / half_width)
    angles = positions.astype(jnp.float32)[:, None] * frequency[None, :]
    cosine = jnp.cos(angles)
    sine_part = jnp.sin(angles)
    first_half = rotary[:, :half_width]
    second_half = rotary[:, half_width:]
    rotated = jnp.concatenate(
        [
            first_half * cosine - second_half * sine_part,
            second_half * cosine + first_half * sine_part,
        ],
        axis=1,
    )
    return jnp.concatenate([compressed, rotated], axis=1).astype(jnp.bfloat16)


def attend(queries, cache_rows, lengths, received, labels, own_rows):
    step_count, req_count = (queries.shape[0], queries.shape[1])
    score_cache = (
        jnp.einsum("trhc,rkc->trhk", queries, cache_rows, preferred_element_type=jnp.float32)
        * SOFT_SCALE
    )
    score_recv = (
        jnp.einsum("trhc,mc->trhm", queries, received, preferred_element_type=jnp.float32)
        * SOFT_SCALE
    )
    score_own = (
        jnp.einsum("trhc,src->trhs", queries, own_rows, preferred_element_type=jnp.float32)
        * SOFT_SCALE
    )
    mask_cache = (jnp.arange(cache_rows.shape[1], dtype=jnp.int32)[None, :] < lengths[:, None])[
        None, :, None, :
    ]
    mask_recv = (labels[None, :] == jnp.arange(req_count, dtype=jnp.int32)[:, None])[
        None, :, None, :
    ]
    step_ids = jnp.arange(step_count, dtype=jnp.int32)
    mask_own = (step_ids[None, :] <= step_ids[:, None])[:, None, None, :]
    score_cache = jnp.where(mask_cache, score_cache, NEG_FILL)
    score_recv = jnp.where(mask_recv, score_recv, NEG_FILL)
    score_own = jnp.where(mask_own, score_own, NEG_FILL)
    highest = jnp.maximum(
        jnp.maximum(score_cache.max(axis=-1), score_recv.max(axis=-1)), score_own.max(axis=-1)
    )[..., None]
    exp_cache = jnp.where(mask_cache, jnp.exp(score_cache - highest), 0.0)
    exp_recv = jnp.where(mask_recv, jnp.exp(score_recv - highest), 0.0)
    exp_own = jnp.where(mask_own, jnp.exp(score_own - highest), 0.0)
    denominator = (
        exp_cache.sum(axis=-1, keepdims=True)
        + exp_recv.sum(axis=-1, keepdims=True)
        + exp_own.sum(axis=-1, keepdims=True)
    )
    prob_cache = (exp_cache / denominator).astype(jnp.bfloat16)
    prob_recv = (exp_recv / denominator).astype(jnp.bfloat16)
    prob_own = (exp_own / denominator).astype(jnp.bfloat16)
    result = jnp.einsum(
        "trhk,rkc->trhc", prob_cache, cache_rows[:, :, :KV_RANK], preferred_element_type=jnp.float32
    )
    result = result + jnp.einsum(
        "trhm,mc->trhc", prob_recv, received[:, :KV_RANK], preferred_element_type=jnp.float32
    )
    result = result + jnp.einsum(
        "trhs,src->trhc", prob_own, own_rows[:, :, :KV_RANK], preferred_element_type=jnp.float32
    )
    return result.astype(jnp.bfloat16)


PLANE = 8
SLAB = 16
TILE = 512


def place_rows(destination, payload, dest_count, capacity):
    dest_ids = jnp.arange(dest_count, dtype=jnp.int32)
    onehot = (destination[:, None] == dest_ids[None, :]).astype(jnp.int32)
    earlier = jnp.cumsum(onehot, axis=0) - onehot
    target = destination * capacity + jnp.sum(earlier * onehot, axis=1)
    select = jnp.arange(dest_count * capacity, dtype=jnp.int32)[:, None] == target[None, :]
    placed = jnp.dot(
        select.astype(jnp.bfloat16), payload, preferred_element_type=jnp.float32
    ).astype(jnp.bfloat16)
    return placed.reshape(dest_count, capacity, payload.shape[1])


def exchange_kernel(
    expert_count,
    w_ref, tok_ref, pre_hbm, dec_ref, gate_hbm, up_hbm, down_hbm,
    proj_ref, back_ref,
    weight, tokens, pre, gate, up, down, accum, hidden, part,
    from_sib, from_a, from_b, sum_a, sum_d, own_sum, sum_b, total, back,
    zs, zr, ps, pr, local, ss, sr, as_, ar, bs, br, fs, fr,
):
    E = expert_count
    me = lax.axis_index("ep")
    e0 = me // PLANE
    j = me % PLANE
    b0, b1, b2 = j % 2, (j // 2) % 2, j // 4
    dx = 2 - 4 * b1
    dy = 4 - 8 * b2
    ds = 1 - 2 * b0
    da = dx * (1 - b0) + dy * b0
    db = dx * b0 + dy * (1 - b0)
    jS, jA, jB, jD = j + ds, j + da, j + db, j + dx + dy
    sA, sB, sD = jS + db, jS + da, jS + dx + dy
    base = e0 * PLANE
    half = tok_ref.shape[2]

    def remote(src, dst, send, recv, device):
        return pltpu.make_async_remote_copy(
            src_ref=src, dst_ref=dst, send_sem=send, recv_sem=recv,
            device_id={"ep": device}, device_id_type=pl.DeviceIdType.MESH,
        )

    loads = [
        pltpu.make_async_copy(w_ref, weight.at[e0, j], local.at[0]),
        pltpu.make_async_copy(tok_ref.at[e0], tokens.at[e0, j], local.at[1]),
        pltpu.make_async_copy(gate_hbm, gate, local.at[2]),
        pltpu.make_async_copy(up_hbm, up, local.at[3]),
        pltpu.make_async_copy(pre_hbm, pre, local.at[4]),
        pltpu.make_async_copy(down_hbm, down, local.at[5]),
    ]
    for load in loads:
        load.start()

    barrier = pltpu.get_barrier_semaphore()
    for k in range(1, E):
        pl.semaphore_signal(
            barrier, inc=1, device_id={"ep": ((e0 + k) % E) * PLANE + j},
            device_id_type=pl.DeviceIdType.MESH,
        )
    for peer in (jS, jA, jB):
        pl.semaphore_signal(
            barrier, inc=1, device_id={"ep": base + peer},
            device_id_type=pl.DeviceIdType.MESH,
        )
    pl.semaphore_wait(barrier, E - 1 + 3)

    def column_send(kind, e):
        source = tok_ref.at[e] if kind == 0 else w_ref
        buffer = tokens if kind == 0 else weight
        return remote(
            source, buffer.at[e0, j], zs.at[kind, e], zr.at[kind, e0], e * PLANE + j
        )

    def column_recv(kind, e):
        source = tok_ref.at[e] if kind == 0 else w_ref
        buffer = tokens if kind == 0 else weight
        return remote(
            source, buffer.at[e, j], zs.at[kind, e], zr.at[kind, e], e * PLANE + j
        )

    for k in range(1, E):
        e = (e0 + k) % E
        column_send(0, e).start()
        column_send(1, e).start()
    loads[0].wait()
    loads[1].wait()

    def plane_send(kind, e, which):
        buffer = tokens if kind == 0 else weight
        block = (j, j, j, jA, jA, jB, jD)[which]
        peer = (jA, jB, jS, jB, jS, jS, jS)[which]
        ref = buffer.at[e, block]
        return remote(ref, ref, ps.at[kind, e, which], pr.at[kind, e, which], base + peer)

    def plane_recv(kind, e, which):
        buffer = tokens if kind == 0 else weight
        block = (jA, jB, jS, jD, sA, sB, sD)[which]
        peer = (jA, jB, jS, jB, jS, jS, jS)[which]
        ref = buffer.at[e, block]
        return remote(ref, ref, ps.at[kind, e, which], pr.at[kind, e, which], base + peer)

    def expert_in(e):
        @pl.loop(0, half // TILE)
        def _(t):
            first = pl.multiple_of(t * TILE, TILE)
            second = pl.multiple_of(half + t * TILE, TILE)
            x = tokens[e, :, :, pl.ds(first, TILE)].reshape(PLANE * SLAB, TILE)
            for at, (matrix, start) in enumerate(
                ((gate, first), (gate, second), (up, first), (up, second))
            ):
                product = jnp.dot(
                    x, matrix[pl.ds(start, TILE), :], preferred_element_type=jnp.float32
                )
                accum[at] = jnp.where(t == 0, 0.0, accum[at]) + product

        def joined(at):
            low = accum[at].reshape(PLANE, SLAB, -1)[:, : SLAB // 2]
            high = accum[at + 1].reshape(PLANE, SLAB, -1)[:, SLAB // 2 :]
            return (low + high).reshape(PLANE * SLAB // 2, -1)

        hidden[e] = (jax.nn.silu(joined(0)) * joined(2)).astype(jnp.bfloat16)

    def project():
        pre_count = pre.shape[0]
        depth = pre.shape[1] // E

        @pl.loop(0, E)
        def _(e):
            for which in (2, 4, 5, 6):
                plane_recv(1, e, which).wait_recv()

        @pl.loop(0, E)
        def _(e):
            block = weight[e].reshape(depth, -1)
            columns = pl.ds(pl.multiple_of(e * depth, 128), depth)
            for rows, offset in ((pre, 0), (dec_ref, pre_count)):
                place = pl.ds(offset, rows.shape[0])
                product = jnp.dot(
                    rows[:, columns], block, preferred_element_type=jnp.float32
                )
                proj_ref[place, :] = jnp.where(e == 0, 0.0, proj_ref[place, :]) + product

    def sib_send(e, which):
        block = (jS, sA, sB, sD)[which]
        return remote(
            part.at[e, block], from_sib.at[e, which], ss.at[e, which], sr.at[e, which], base + jS
        )

    def a_send(e, which):
        source = (sum_a, sum_d)[which]
        return remote(
            source.at[e], from_a.at[e, which], as_.at[e, which], ar.at[e, which], base + jA
        )

    def b_send(e):
        return remote(sum_b.at[e], from_b.at[e], bs.at[e], br.at[e], base + jB)

    def back_send(e):
        return remote(total.at[e], back.at[e0], fs.at[e], fr.at[e0], e * PLANE + j)

    def back_recv(e):
        return remote(total.at[e], back.at[e], fs.at[e], fr.at[e], e * PLANE + j)

    def wide(ref):
        return ref.astype(jnp.float32)

    def spread(kind, e):
        for which in (0, 1, 2):
            plane_send(kind, e, which).start()

    def relay(kind, e):
        plane_recv(kind, e, 0).wait_recv()
        plane_send(kind, e, 3).start()
        plane_send(kind, e, 4).start()
        plane_recv(kind, e, 1).wait_recv()
        plane_send(kind, e, 5).start()

    def finish(kind, e):
        plane_recv(kind, e, 3).wait_recv()
        plane_send(kind, e, 6).start()

    def expert_out(e):
        @pl.loop(0, half // TILE)
        def _(c):
            first = pl.multiple_of(c * TILE, TILE)
            second = pl.multiple_of(half + c * TILE, TILE)
            low, high = (
                jnp.dot(
                    hidden[e], down[:, pl.ds(start, TILE)],
                    preferred_element_type=jnp.float32,
                ).reshape(PLANE, SLAB // 2, TILE)
                for start in (first, second)
            )
            part[e, :, :, pl.ds(first, TILE)] = jnp.concatenate([low, high], axis=1).astype(
                jnp.bfloat16
            )

    spread(0, e0)
    spread(1, e0)
    loads[2].wait()
    loads[3].wait()
    loads[4].wait()
    loads[5].wait()

    def stage(t, lag, first=0):
        def wrap(body):
            k = t - lag

            @pl.when((k >= first) & (k < E))
            def _():
                body((e0 + E - k) % E)

        return wrap

    @pl.loop(1, E + 6)
    def _(t):
        @stage(t, 0, 1)
        def _(e):
            column_recv(0, e).wait_recv()
            spread(0, e)

        @stage(t, 1)
        def _(e):
            relay(0, e)

        @stage(t, 1, 1)
        def _(e):
            column_recv(1, e).wait_recv()
            spread(1, e)

        @stage(t, 2)
        def _(e):
            finish(0, e)

        @stage(t, 3)
        def _(e):
            for which in (2, 4, 5, 6):
                plane_recv(0, e, which).wait_recv()
            expert_in(e)
            expert_out(e)
            for which in (1, 3, 2, 0):
                sib_send(e, which).start()

        @stage(t, 4)
        def _(e):
            sib_send(e, 1).wait_recv()
            sum_a[e] = (wide(part[e, jA]) + wide(from_sib[e, 1])).astype(jnp.bfloat16)
            a_send(e, 0).start()
            sib_send(e, 3).wait_recv()
            sum_d[e] = (wide(part[e, jD]) + wide(from_sib[e, 3])).astype(jnp.bfloat16)
            a_send(e, 1).start()

        @stage(t, 5)
        def _(e):
            sib_send(e, 0).wait_recv()
            sib_send(e, 2).wait_recv()
            a_send(e, 1).wait_recv()
            sum_b[e] = (
                wide(part[e, jB]) + wide(from_sib[e, 2]) + wide(from_a[e, 1])
            ).astype(jnp.bfloat16)
            b_send(e).start()
            a_send(e, 0).wait_recv()
            own_sum[e] = wide(part[e, j]) + wide(from_sib[e, 0]) + wide(from_a[e, 0])

        @stage(t, 6)
        def _(e):
            b_send(e).wait_recv()
            total[e] = (own_sum[e] + wide(from_b[e])).astype(jnp.bfloat16)

            @pl.when(t > 6)
            def _():
                back_send(e).start()

        @stage(t, 4)
        def _(e):
            relay(1, e)

        @stage(t, 6)
        def _(e):
            finish(1, e)

    project()
    back_ref[e0] = wide(total[e0])

    @pl.loop(1, E)
    def _(k):
        e = (e0 + k) % E
        back_recv(e).wait_recv()
        back_ref[e] = wide(back[e])

    @pl.loop(0, E)
    def _(e):
        for kind in (0, 1):
            for which in range(7):
                plane_send(kind, e, which).wait_send()
        for which in range(4):
            sib_send(e, which).wait_send()
        a_send(e, 0).wait_send()
        a_send(e, 1).wait_send()
        b_send(e).wait_send()

    @pl.loop(1, E)
    def _(k):
        e = (e0 + k) % E
        column_send(0, e).wait_send()
        column_send(1, e).wait_send()
        back_send(e).wait_send()


def exchange(proj_weight, packed, prefill_rows, decode_flat, gate_weight, up_weight, down_weight):
    E, _, half = packed.shape
    width = 2 * half
    shard, latent_width = proj_weight.shape
    hidden_dev = gate_weight.shape[1]
    rows = prefill_rows.shape[0] + decode_flat.shape[0]
    bf16 = jnp.bfloat16
    block = (E, SLAB, half)
    dma = pltpu.SemaphoreType.DMA
    vmem = pl.BlockSpec(memory_space=pltpu.VMEM)
    hbm = pl.BlockSpec(memory_space=pl.ANY)
    return pl.pallas_call(
        functools.partial(exchange_kernel, E),
        out_shape=(
            jax.ShapeDtypeStruct((rows, latent_width), jnp.float32),
            jax.ShapeDtypeStruct(block, jnp.float32),
        ),
        in_specs=[vmem, vmem, hbm, vmem, hbm, hbm, hbm],
        out_specs=(vmem, vmem),
        scratch_shapes=[
            pltpu.VMEM((E, PLANE, shard, latent_width), bf16),
            pltpu.VMEM((E, PLANE, SLAB, half), bf16),
            pltpu.VMEM(prefill_rows.shape, bf16),
            pltpu.VMEM(gate_weight.shape, bf16),
            pltpu.VMEM(up_weight.shape, bf16),
            pltpu.VMEM(down_weight.shape, bf16),
            pltpu.VMEM((4, PLANE * SLAB, hidden_dev), jnp.float32),
            pltpu.VMEM((E, PLANE * SLAB // 2, hidden_dev), bf16),
            pltpu.VMEM((E, PLANE, SLAB, half), bf16),
            pltpu.VMEM((E, 4, SLAB, half), bf16),
            pltpu.VMEM((E, 2, SLAB, half), bf16),
            pltpu.VMEM(block, bf16),
            pltpu.VMEM(block, bf16),
            pltpu.VMEM(block, bf16),
            pltpu.VMEM(block, jnp.float32),
            pltpu.VMEM(block, bf16),
            pltpu.VMEM(block, bf16),
            pltpu.VMEM(block, bf16),
            dma((2, E)), dma((2, E)), dma((2, E, 7)), dma((2, E, 7)), dma((6,)),
            dma((E, 4)), dma((E, 4)), dma((E, 2)), dma((E, 2)), dma((E,)), dma((E,)),
            dma((E,)), dma((E,)),
        ],
        compiler_params=pltpu.CompilerParams(
            collective_id=0, has_side_effects=True, vmem_limit_bytes=56 * 1024 * 1024
        ),
    )(proj_weight, packed, prefill_rows, decode_flat, gate_weight, up_weight, down_weight)


def pack(normed, routes, gate_scores, expert_count, capacity):
    step_count, req_count, width = normed.shape
    chosen = routes.reshape(step_count, req_count * TOP)
    onehot = (chosen[:, :, None] == jnp.arange(expert_count, dtype=jnp.int32)).astype(jnp.int32)
    earlier = jnp.cumsum(onehot, axis=1) - onehot
    slots = step_count * capacity
    step_ids = jnp.arange(step_count, dtype=jnp.int32)[:, None]
    row = chosen * slots + step_ids * capacity + jnp.sum(earlier * onehot, axis=2)
    row = row.reshape(step_count * req_count, TOP)
    match = row[:, :, None] == jnp.arange(expert_count * slots, dtype=jnp.int32)
    mixing = jnp.sum(jnp.where(match, gate_scores.reshape(-1, TOP)[:, :, None], 0.0), axis=1)
    select = jnp.any(match, axis=1).astype(jnp.bfloat16)
    packed = jnp.einsum(
        "tr,td->rd", select, normed.reshape(-1, width), preferred_element_type=jnp.float32
    ).astype(jnp.bfloat16)
    packed = packed.reshape(expert_count, slots, 2, width // 2).transpose(0, 2, 1, 3)
    return packed.reshape(expert_count, 2 * slots, width // 2), mixing


def shards(
    prefill_rows,
    proj_weight,
    latent_gain,
    prefill_position,
    row_owner,
    row_request,
    latent_cache,
    cache_len,
    queries,
    decode_rows,
    moe_gain,
    routes,
    gate_scores,
    gate_weight,
    up_weight,
    down_weight,
):
    ep_count = lax.axis_size("ep")
    pre_count = prefill_rows.shape[0]
    step_count, req_count, width = decode_rows.shape
    latent_width = proj_weight.shape[1]
    expert_count = ep_count // PLANE
    assert MOE_FF == PLANE * gate_weight.shape[1]
    capacity = max(2, req_count * TOP // expert_count)
    assert step_count * capacity * 2 == SLAB

    token_rows = decode_rows.astype(jnp.float32)
    factor = lax.rsqrt(jnp.mean(token_rows * token_rows, axis=2, keepdims=True) + NORM_EPS)
    normed = (token_rows * factor * moe_gain[None, None, :]).astype(jnp.bfloat16)
    packed, mixing = pack(normed, routes, gate_scores, expert_count, capacity)

    projected, back = exchange(
        proj_weight,
        packed,
        prefill_rows,
        decode_rows.reshape(step_count * req_count, width),
        gate_weight,
        up_weight,
        down_weight,
    )

    decode_position = (
        cache_len[None, :] + jnp.arange(step_count, dtype=jnp.int32)[:, None]
    ).reshape(-1)
    positions = jnp.concatenate([prefill_position, decode_position], axis=0)
    latent = latent_rows(projected, positions, latent_gain)
    own_rows = latent[pre_count:].reshape(step_count, req_count, latent_width)
    send_cap = max(2, 2 * pre_count // ep_count)
    payload = jnp.concatenate(
        [latent[:pre_count], (row_request + 1).astype(jnp.bfloat16)[:, None]], axis=1
    )
    placed = place_rows(row_owner[:, 0], payload, ep_count, send_cap)
    received = lax.all_to_all(placed, "ep", split_axis=0, concat_axis=0, tiled=True)
    received = received.reshape(-1, latent_width + 1)
    attn_out = attend(
        queries,
        latent_cache,
        cache_len,
        received[:, :latent_width],
        received[:, latent_width].astype(jnp.int32) - 1,
        own_rows,
    )
    slots = step_count * capacity
    expert_rows = back.reshape(expert_count, 2, slots, width // 2).transpose(0, 2, 1, 3)
    moe_out = jnp.dot(
        mixing,
        expert_rows.reshape(expert_count * slots, width),
        precision=lax.Precision.HIGHEST,
        preferred_element_type=jnp.float32,
    )
    moe_out = moe_out.reshape(step_count, req_count, width).astype(jnp.bfloat16)
    return (attn_out, moe_out)


def solution(mesh):
    in_specs = (
        P(("groups", "ep"), None),
        P("ep", None),
        P(),
        P(("groups", "ep")),
        P(("groups", "ep"), None),
        P(("groups", "ep")),
        P(("groups", "ep"), None, None),
        P(("groups", "ep")),
        P(None, ("groups", "ep"), None, None),
        P(None, ("groups", "ep"), None),
        P(),
        P(None, ("groups", "ep"), None),
        P(None, ("groups", "ep"), None),
        P(None, "ep"),
        P(None, "ep"),
        P("ep", None),
    )
    out_specs = (P(None, ("groups", "ep"), None, None), P(None, ("groups", "ep"), None))
    return jax.shard_map(shards, mesh=mesh, in_specs=in_specs, out_specs=out_specs, check_vma=False)
```

```python
import functools

import jax
import jax.numpy as jnp
from jax import lax
from jax.experimental import pallas as pl
from jax.experimental.pallas import tpu as pltpu
from jax.sharding import PartitionSpec as P

KV_RANK = 512
MOE_FF = 1024
TOP = 2


NORM_EPS = 1e-06
SOFT_SCALE = 192.0 ** (-0.5)
NEG_FILL = -1e30


def latent_rows(projected, positions, latent_gain):
    compressed = projected[:, :KV_RANK]
    rotary = projected[:, KV_RANK:]
    factor = lax.rsqrt(jnp.mean(compressed * compressed, axis=1, keepdims=True) + NORM_EPS)
    compressed = compressed * factor * latent_gain[None, :]
    half_width = rotary.shape[1] // 2
    frequency = 10000.0 ** (-jnp.arange(half_width, dtype=jnp.float32) / half_width)
    angles = positions.astype(jnp.float32)[:, None] * frequency[None, :]
    cosine = jnp.cos(angles)
    sine_part = jnp.sin(angles)
    first_half = rotary[:, :half_width]
    second_half = rotary[:, half_width:]
    rotated = jnp.concatenate(
        [
            first_half * cosine - second_half * sine_part,
            second_half * cosine + first_half * sine_part,
        ],
        axis=1,
    )
    return jnp.concatenate([compressed, rotated], axis=1).astype(jnp.bfloat16)


def attend(queries, cache_rows, lengths, received, labels, own_rows):
    step_count, req_count = (queries.shape[0], queries.shape[1])
    score_cache = (
        jnp.einsum("trhc,rkc->trhk", queries, cache_rows, preferred_element_type=jnp.float32)
        * SOFT_SCALE
    )
    score_recv = (
        jnp.einsum("trhc,mc->trhm", queries, received, preferred_element_type=jnp.float32)
        * SOFT_SCALE
    )
    score_own = (
        jnp.einsum("trhc,src->trhs", queries, own_rows, preferred_element_type=jnp.float32)
        * SOFT_SCALE
    )
    mask_cache = (jnp.arange(cache_rows.shape[1], dtype=jnp.int32)[None, :] < lengths[:, None])[
        None, :, None, :
    ]
    mask_recv = (labels[None, :] == jnp.arange(req_count, dtype=jnp.int32)[:, None])[
        None, :, None, :
    ]
    step_ids = jnp.arange(step_count, dtype=jnp.int32)
    mask_own = (step_ids[None, :] <= step_ids[:, None])[:, None, None, :]
    score_cache = jnp.where(mask_cache, score_cache, NEG_FILL)
    score_recv = jnp.where(mask_recv, score_recv, NEG_FILL)
    score_own = jnp.where(mask_own, score_own, NEG_FILL)
    highest = jnp.maximum(
        jnp.maximum(score_cache.max(axis=-1), score_recv.max(axis=-1)), score_own.max(axis=-1)
    )[..., None]
    exp_cache = jnp.where(mask_cache, jnp.exp(score_cache - highest), 0.0)
    exp_recv = jnp.where(mask_recv, jnp.exp(score_recv - highest), 0.0)
    exp_own = jnp.where(mask_own, jnp.exp(score_own - highest), 0.0)
    denominator = (
        exp_cache.sum(axis=-1, keepdims=True)
        + exp_recv.sum(axis=-1, keepdims=True)
        + exp_own.sum(axis=-1, keepdims=True)
    )
    prob_cache = (exp_cache / denominator).astype(jnp.bfloat16)
    prob_recv = (exp_recv / denominator).astype(jnp.bfloat16)
    prob_own = (exp_own / denominator).astype(jnp.bfloat16)
    result = jnp.einsum(
        "trhk,rkc->trhc", prob_cache, cache_rows[:, :, :KV_RANK], preferred_element_type=jnp.float32
    )
    result = result + jnp.einsum(
        "trhm,mc->trhc", prob_recv, received[:, :KV_RANK], preferred_element_type=jnp.float32
    )
    result = result + jnp.einsum(
        "trhs,src->trhc", prob_own, own_rows[:, :, :KV_RANK], preferred_element_type=jnp.float32
    )
    return result.astype(jnp.bfloat16)


PLANE = 8
SLAB = 16
TILE = 512


def place_rows(destination, payload, dest_count, capacity):
    dest_ids = jnp.arange(dest_count, dtype=jnp.int32)
    onehot = (destination[:, None] == dest_ids[None, :]).astype(jnp.int32)
    earlier = jnp.cumsum(onehot, axis=0) - onehot
    target = destination * capacity + jnp.sum(earlier * onehot, axis=1)
    select = jnp.arange(dest_count * capacity, dtype=jnp.int32)[:, None] == target[None, :]
    placed = jnp.dot(
        select.astype(jnp.bfloat16), payload, preferred_element_type=jnp.float32
    ).astype(jnp.bfloat16)
    return placed.reshape(dest_count, capacity, payload.shape[1])


def exchange_kernel(
    expert_count,
    w_ref, tok_ref, pre_hbm, dec_ref, gate_hbm, up_hbm, down_hbm,
    proj_ref, back_ref,
    weight, tokens, pre, gate, up, down, accum, hidden, part,
    from_sib, from_a, from_b, sum_a, sum_d, own_sum, sum_b, total, back,
    zs, zr, ps, pr, local, ss, sr, as_, ar, bs, br, fs, fr,
):
    E = expert_count
    me = lax.axis_index("ep")
    e0 = me // PLANE
    j = me % PLANE
    b0, b1, b2 = j % 2, (j // 2) % 2, j // 4
    dx = 2 - 4 * b1
    dy = 4 - 8 * b2
    ds = 1 - 2 * b0
    da = dx * (1 - b0) + dy * b0
    db = dx * b0 + dy * (1 - b0)
    jS, jA, jB, jD = j + ds, j + da, j + db, j + dx + dy
    sA, sB, sD = jS + db, jS + da, jS + dx + dy
    base = e0 * PLANE
    half = tok_ref.shape[2]

    def remote(src, dst, send, recv, device):
        return pltpu.make_async_remote_copy(
            src_ref=src, dst_ref=dst, send_sem=send, recv_sem=recv,
            device_id={"ep": device}, device_id_type=pl.DeviceIdType.MESH,
        )

    loads = [
        pltpu.make_async_copy(w_ref, weight.at[e0, j], local.at[0]),
        pltpu.make_async_copy(tok_ref.at[e0], tokens.at[e0, j], local.at[1]),
        pltpu.make_async_copy(gate_hbm, gate, local.at[2]),
        pltpu.make_async_copy(up_hbm, up, local.at[3]),
        pltpu.make_async_copy(pre_hbm, pre, local.at[4]),
        pltpu.make_async_copy(down_hbm, down, local.at[5]),
    ]
    for load in loads:
        load.start()

    barrier = pltpu.get_barrier_semaphore()
    for k in range(1, E):
        pl.semaphore_signal(
            barrier, inc=1, device_id={"ep": ((e0 + k) % E) * PLANE + j},
            device_id_type=pl.DeviceIdType.MESH,
        )
    for peer in (jS, jA, jB):
        pl.semaphore_signal(
            barrier, inc=1, device_id={"ep": base + peer},
            device_id_type=pl.DeviceIdType.MESH,
        )
    pl.semaphore_wait(barrier, E - 1 + 3)

    def column_send(kind, e):
        source = tok_ref.at[e] if kind == 0 else w_ref
        buffer = tokens if kind == 0 else weight
        return remote(
            source, buffer.at[e0, j], zs.at[kind, e], zr.at[kind, e0], e * PLANE + j
        )

    def column_recv(kind, e):
        source = tok_ref.at[e] if kind == 0 else w_ref
        buffer = tokens if kind == 0 else weight
        return remote(
            source, buffer.at[e, j], zs.at[kind, e], zr.at[kind, e], e * PLANE + j
        )

    for k in range(1, E):
        e = (e0 + k) % E
        column_send(0, e).start()
        column_send(1, e).start()
    loads[0].wait()
    loads[1].wait()

    def plane_send(kind, e, which):
        buffer = tokens if kind == 0 else weight
        block = (j, j, j, jA, jA, jB, jD)[which]
        peer = (jA, jB, jS, jB, jS, jS, jS)[which]
        ref = buffer.at[e, block]
        return remote(ref, ref, ps.at[kind, e, which], pr.at[kind, e, which], base + peer)

    def plane_recv(kind, e, which):
        buffer = tokens if kind == 0 else weight
        block = (jA, jB, jS, jD, sA, sB, sD)[which]
        peer = (jA, jB, jS, jB, jS, jS, jS)[which]
        ref = buffer.at[e, block]
        return remote(ref, ref, ps.at[kind, e, which], pr.at[kind, e, which], base + peer)

    def expert_in(e):
        @pl.loop(0, half // TILE)
        def _(t):
            first = pl.multiple_of(t * TILE, TILE)
            second = pl.multiple_of(half + t * TILE, TILE)
            x = tokens[e, :, :, pl.ds(first, TILE)].reshape(PLANE * SLAB, TILE)
            for at, (matrix, start) in enumerate(
                ((gate, first), (gate, second), (up, first), (up, second))
            ):
                product = jnp.dot(
                    x, matrix[pl.ds(start, TILE), :], preferred_element_type=jnp.float32
                )
                accum[at] = jnp.where(t == 0, 0.0, accum[at]) + product

        def joined(at):
            low = accum[at].reshape(PLANE, SLAB, -1)[:, : SLAB // 2]
            high = accum[at + 1].reshape(PLANE, SLAB, -1)[:, SLAB // 2 :]
            return (low + high).reshape(PLANE * SLAB // 2, -1)

        hidden[e] = (jax.nn.silu(joined(0)) * joined(2)).astype(jnp.bfloat16)

    def project():
        pre_count = pre.shape[0]
        depth = pre.shape[1] // E

        @pl.loop(0, E)
        def _(e):
            for which in (2, 4, 5, 6):
                plane_recv(1, e, which).wait_recv()

        @pl.loop(0, E)
        def _(e):
            block = weight[e].reshape(depth, -1)
            columns = pl.ds(pl.multiple_of(e * depth, 128), depth)
            for rows, offset in ((pre, 0), (dec_ref, pre_count)):
                place = pl.ds(offset, rows.shape[0])
                product = jnp.dot(
                    rows[:, columns], block, preferred_element_type=jnp.float32
                )
                proj_ref[place, :] = jnp.where(e == 0, 0.0, proj_ref[place, :]) + product

    def sib_send(e, which):
        block = (jS, sA, sB, sD)[which]
        return remote(
            part.at[e, block], from_sib.at[e, which], ss.at[e, which], sr.at[e, which], base + jS
        )

    def a_send(e, which):
        source = (sum_a, sum_d)[which]
        return remote(
            source.at[e], from_a.at[e, which], as_.at[e, which], ar.at[e, which], base + jA
        )

    def b_send(e):
        return remote(sum_b.at[e], from_b.at[e], bs.at[e], br.at[e], base + jB)

    def back_send(e):
        return remote(total.at[e], back.at[e0], fs.at[e], fr.at[e0], e * PLANE + j)

    def back_recv(e):
        return remote(total.at[e], back.at[e], fs.at[e], fr.at[e], e * PLANE + j)

    def wide(ref):
        return ref.astype(jnp.float32)

    def spread(kind, e):
        for which in (0, 1, 2):
            plane_send(kind, e, which).start()

    def relay(kind, e):
        plane_recv(kind, e, 0).wait_recv()
        plane_send(kind, e, 3).start()
        plane_send(kind, e, 4).start()
        plane_recv(kind, e, 1).wait_recv()
        plane_send(kind, e, 5).start()

    def finish(kind, e):
        plane_recv(kind, e, 3).wait_recv()
        plane_send(kind, e, 6).start()

    def expert_out(e):
        @pl.loop(0, half // TILE)
        def _(c):
            first = pl.multiple_of(c * TILE, TILE)
            second = pl.multiple_of(half + c * TILE, TILE)
            low, high = (
                jnp.dot(
                    hidden[e], down[:, pl.ds(start, TILE)],
                    preferred_element_type=jnp.float32,
                ).reshape(PLANE, SLAB // 2, TILE)
                for start in (first, second)
            )
            part[e, :, :, pl.ds(first, TILE)] = jnp.concatenate([low, high], axis=1).astype(
                jnp.bfloat16
            )

    spread(0, e0)
    spread(1, e0)
    loads[2].wait()
    loads[3].wait()
    loads[4].wait()
    loads[5].wait()

    def stage(t, lag, first=0):
        def wrap(body):
            k = t - lag

            @pl.when((k >= first) & (k < E))
            def _():
                body((e0 + E - k) % E)

        return wrap

    @pl.loop(1, E + 6)
    def _(t):
        @stage(t, 0, 1)
        def _(e):
            column_recv(0, e).wait_recv()
            spread(0, e)

        @stage(t, 1)
        def _(e):
            relay(0, e)

        @stage(t, 1, 1)
        def _(e):
            column_recv(1, e).wait_recv()
            spread(1, e)

        @stage(t, 2)
        def _(e):
            finish(0, e)

        @stage(t, 3)
        def _(e):
            for which in (2, 4, 5, 6):
                plane_recv(0, e, which).wait_recv()
            expert_in(e)
            expert_out(e)
            for which in (1, 3, 2, 0):
                sib_send(e, which).start()

        @stage(t, 4)
        def _(e):
            sib_send(e, 1).wait_recv()
            sum_a[e] = (wide(part[e, jA]) + wide(from_sib[e, 1])).astype(jnp.bfloat16)
            a_send(e, 0).start()
            sib_send(e, 3).wait_recv()
            sum_d[e] = (wide(part[e, jD]) + wide(from_sib[e, 3])).astype(jnp.bfloat16)
            a_send(e, 1).start()

        @stage(t, 5)
        def _(e):
            sib_send(e, 0).wait_recv()
            sib_send(e, 2).wait_recv()
            a_send(e, 1).wait_recv()
            sum_b[e] = (
                wide(part[e, jB]) + wide(from_sib[e, 2]) + wide(from_a[e, 1])
            ).astype(jnp.bfloat16)
            b_send(e).start()
            a_send(e, 0).wait_recv()
            own_sum[e] = wide(part[e, j]) + wide(from_sib[e, 0]) + wide(from_a[e, 0])

        @stage(t, 6)
        def _(e):
            b_send(e).wait_recv()
            total[e] = (own_sum[e] + wide(from_b[e])).astype(jnp.bfloat16)

            @pl.when(t > 6)
            def _():
                back_send(e).start()

        @stage(t, 4)
        def _(e):
            relay(1, e)

        @stage(t, 6)
        def _(e):
            finish(1, e)

    project()
    back_ref[e0] = wide(total[e0])

    @pl.loop(1, E)
    def _(k):
        e = (e0 + k) % E
        back_recv(e).wait_recv()
        back_ref[e] = wide(back[e])

    @pl.loop(0, E)
    def _(e):
        for kind in (0, 1):
            for which in range(7):
                plane_send(kind, e, which).wait_send()
        for which in range(4):
            sib_send(e, which).wait_send()
        a_send(e, 0).wait_send()
        a_send(e, 1).wait_send()
        b_send(e).wait_send()

    @pl.loop(1, E)
    def _(k):
        e = (e0 + k) % E
        column_send(0, e).wait_send()
        column_send(1, e).wait_send()
        back_send(e).wait_send()


def exchange(proj_weight, packed, prefill_rows, decode_flat, gate_weight, up_weight, down_weight):
    E, _, half = packed.shape
    width = 2 * half
    shard, latent_width = proj_weight.shape
    hidden_dev = gate_weight.shape[1]
    rows = prefill_rows.shape[0] + decode_flat.shape[0]
    bf16 = jnp.bfloat16
    block = (E, SLAB, half)
    dma = pltpu.SemaphoreType.DMA
    vmem = pl.BlockSpec(memory_space=pltpu.VMEM)
    hbm = pl.BlockSpec(memory_space=pl.ANY)
    return pl.pallas_call(
        functools.partial(exchange_kernel, E),
        out_shape=(
            jax.ShapeDtypeStruct((rows, latent_width), jnp.float32),
            jax.ShapeDtypeStruct(block, jnp.float32),
        ),
        in_specs=[vmem, vmem, hbm, vmem, hbm, hbm, hbm],
        out_specs=(vmem, vmem),
        scratch_shapes=[
            pltpu.VMEM((E, PLANE, shard, latent_width), bf16),
            pltpu.VMEM((E, PLANE, SLAB, half), bf16),
            pltpu.VMEM(prefill_rows.shape, bf16),
            pltpu.VMEM(gate_weight.shape, bf16),
            pltpu.VMEM(up_weight.shape, bf16),
            pltpu.VMEM(down_weight.shape, bf16),
            pltpu.VMEM((4, PLANE * SLAB, hidden_dev), jnp.float32),
            pltpu.VMEM((E, PLANE * SLAB // 2, hidden_dev), bf16),
            pltpu.VMEM((E, PLANE, SLAB, half), bf16),
            pltpu.VMEM((E, 4, SLAB, half), bf16),
            pltpu.VMEM((E, 2, SLAB, half), bf16),
            pltpu.VMEM(block, bf16),
            pltpu.VMEM(block, bf16),
            pltpu.VMEM(block, bf16),
            pltpu.VMEM(block, jnp.float32),
            pltpu.VMEM(block, bf16),
            pltpu.VMEM(block, bf16),
            pltpu.VMEM(block, bf16),
            dma((2, E)), dma((2, E)), dma((2, E, 7)), dma((2, E, 7)), dma((6,)),
            dma((E, 4)), dma((E, 4)), dma((E, 2)), dma((E, 2)), dma((E,)), dma((E,)),
            dma((E,)), dma((E,)),
        ],
        compiler_params=pltpu.CompilerParams(
            collective_id=0, has_side_effects=True, vmem_limit_bytes=56 * 1024 * 1024
        ),
    )(proj_weight, packed, prefill_rows, decode_flat, gate_weight, up_weight, down_weight)


def slot_match(routes, expert_count, capacity):
    step_count, req_count, _ = routes.shape
    chosen = routes.reshape(step_count, req_count * TOP)
    order = jnp.arange(req_count * TOP, dtype=jnp.int32)
    same = (chosen[:, :, None] == chosen[:, None, :]) & (order[None, :] < order[:, None])
    slots = step_count * capacity
    step_ids = jnp.arange(step_count, dtype=jnp.int32)[:, None]
    row = chosen * slots + step_ids * capacity + jnp.sum(same.astype(jnp.int32), axis=2)
    row = row.reshape(step_count * req_count, TOP)
    return row[:, :, None] == jnp.arange(expert_count * slots, dtype=jnp.int32)


def pack(normed, routes, expert_count, capacity):
    width = normed.shape[2]
    slots = normed.shape[0] * capacity
    select = jnp.any(slot_match(routes, expert_count, capacity), axis=1).astype(jnp.bfloat16)
    packed = jnp.einsum(
        "tr,td->rd", select, normed.reshape(-1, width), preferred_element_type=jnp.float32
    ).astype(jnp.bfloat16)
    packed = packed.reshape(expert_count, slots, 2, width // 2).transpose(0, 2, 1, 3)
    return packed.reshape(expert_count, 2 * slots, width // 2)


def shards(
    prefill_rows,
    proj_weight,
    latent_gain,
    prefill_position,
    row_owner,
    row_request,
    latent_cache,
    cache_len,
    queries,
    decode_rows,
    moe_gain,
    routes,
    gate_scores,
    gate_weight,
    up_weight,
    down_weight,
):
    ep_count = lax.axis_size("ep")
    pre_count = prefill_rows.shape[0]
    step_count, req_count, width = decode_rows.shape
    latent_width = proj_weight.shape[1]
    expert_count = ep_count // PLANE
    assert MOE_FF == PLANE * gate_weight.shape[1]
    capacity = max(2, req_count * TOP // expert_count)
    assert step_count * capacity * 2 == SLAB

    token_rows = decode_rows.astype(jnp.float32)
    factor = lax.rsqrt(jnp.mean(token_rows * token_rows, axis=2, keepdims=True) + NORM_EPS)
    normed = (token_rows * factor * moe_gain[None, None, :]).astype(jnp.bfloat16)
    packed = pack(normed, routes, expert_count, capacity)

    projected, back = exchange(
        proj_weight,
        packed,
        prefill_rows,
        decode_rows.reshape(step_count * req_count, width),
        gate_weight,
        up_weight,
        down_weight,
    )

    projected, late_routes = lax.optimization_barrier((projected, routes))
    decode_position = (
        cache_len[None, :] + jnp.arange(step_count, dtype=jnp.int32)[:, None]
    ).reshape(-1)
    positions = jnp.concatenate([prefill_position, decode_position], axis=0)
    latent = latent_rows(projected, positions, latent_gain)
    own_rows = latent[pre_count:].reshape(step_count, req_count, latent_width)
    send_cap = max(2, 2 * pre_count // ep_count)
    payload = jnp.concatenate(
        [latent[:pre_count], (row_request + 1).astype(jnp.bfloat16)[:, None]], axis=1
    )
    placed = place_rows(row_owner[:, 0], payload, ep_count, send_cap)
    received = lax.all_to_all(placed, "ep", split_axis=0, concat_axis=0, tiled=True)
    received = received.reshape(-1, latent_width + 1)
    attn_out = attend(
        queries,
        latent_cache,
        cache_len,
        received[:, :latent_width],
        received[:, latent_width].astype(jnp.int32) - 1,
        own_rows,
    )
    slots = step_count * capacity
    match = slot_match(late_routes, expert_count, capacity)
    mixing = jnp.sum(jnp.where(match, gate_scores.reshape(-1, TOP)[:, :, None], 0.0), axis=1)
    expert_rows = back.reshape(expert_count, 2, slots, width // 2).transpose(0, 2, 1, 3)
    moe_out = jnp.dot(
        mixing,
        expert_rows.reshape(expert_count * slots, width),
        precision=lax.Precision.HIGHEST,
        preferred_element_type=jnp.float32,
    )
    moe_out = moe_out.reshape(step_count, req_count, width).astype(jnp.bfloat16)
    return (attn_out, moe_out)


def solution(mesh):
    in_specs = (
        P(("groups", "ep"), None),
        P("ep", None),
        P(),
        P(("groups", "ep")),
        P(("groups", "ep"), None),
        P(("groups", "ep")),
        P(("groups", "ep"), None, None),
        P(("groups", "ep")),
        P(None, ("groups", "ep"), None, None),
        P(None, ("groups", "ep"), None),
        P(),
        P(None, ("groups", "ep"), None),
        P(None, ("groups", "ep"), None),
        P(None, "ep"),
        P(None, "ep"),
        P("ep", None),
    )
    out_specs = (P(None, ("groups", "ep"), None, None), P(None, ("groups", "ep"), None))
    return jax.shard_map(shards, mesh=mesh, in_specs=in_specs, out_specs=out_specs, check_vma=False)
```
